32 devices in a mesh: img: 8 (over z, y), shot: 4 (over x, core).
Axes of the slice: x: 2, y: 2, z: 4, core: 2. Of those that a mesh axis runs over, the one named last changes fastest.
Arguments:
- shot_green: bfloat16 [2, 3584, 1024], P(None, 'img', 'shot'), may hold values from -6 to 6
- rec_green: bfloat16 [2, 3584, 3584], P(None, 'img'), may hold values from -0.0625 to 0.0625
- model: float32 [3584], P('img'), may hold values from 0.2 to 2
- hadamard_order: int32 [256], replicated, may hold values from 0 to 255, each once
- shot_signs: int32 [1024], P('shot'), may hold values from 0 to 1
Outputs:
- born_data: bfloat16 [2, 3584, 1024], P(None, 'img', 'shot')
The draws below stay inside these ranges and needn't reach their ends.
Inputs may be any that keep to these rules, and one draw needn't show every extreme that they name: `hadamard_order`: each of 0 to 255 once.
All inputs are finite; a program needn't handle non-finite values.
Results may differ from the reference program's by a relative error of at most 0.0049.
Values may be sent and summed in bfloat16 or wider, within the bound.
A program may use at most 128 MiB of HBM per device.

```python
import math
import jax
import jax.numpy as jnp
from jax import lax

SHOT_DEV = 256
IMAGE = 3584
RECEIVERS = 3584
SHOT = 1024
N_SHOT = 4


def with_ends(entries, own_key, low, high):
    spot = [jax.random.randint(jax.random.fold_in(own_key, axis), (), 0, length) for axis, length in enumerate(entries.shape)]
    main_axis = entries.shape.index(max(entries.shape))
    neighbour = spot[:main_axis] + [(spot[main_axis] + 1) % entries.shape[main_axis]] + spot[main_axis + 1:]
    return entries.at[tuple(spot)].set(low).at[tuple(neighbour)].set(high)


def shard_levels(rng, shape, cuts, smallest, high):
    loudness, own = 1.0, jax.random.fold_in(rng, 6)
    for axis_at, parts in cuts:
        heights = jnp.exp(jax.random.uniform(jax.random.fold_in(own, axis_at), (parts,), jnp.float32, smallest / len(cuts), high / len(cuts)))
        loudness = loudness * jnp.repeat(heights, shape[axis_at] // parts).reshape([-1 if axis == axis_at else 1 for axis in range(len(shape))])
    return loudness


def gaussian(key, extent, width, most, cuts=(), held_as=jnp.bfloat16):
    array = width * jax.random.normal(key, extent, jnp.float32)
    if cuts:
        array = array * shard_levels(key, extent, cuts, -0.22, 0.18)
    return jnp.clip(array, -most, most).astype(held_as)


def setup_inputs(seed: int = 0) -> dict:
    key_of = jax.random.split(jax.random.key(seed), 6)
    return {
        "shot_green": gaussian(key_of[0], (2, IMAGE, SHOT), 1.0, 6.0, ((1, 8), (2, 4))),
        "rec_green": gaussian(key_of[1], (2, RECEIVERS, IMAGE), (2 * IMAGE) ** -0.5, 0.0625, ((1, 8),)),
        "model": jnp.clip(jnp.exp(math.log(2.0) - 2.3025851 * jax.random.uniform(key_of[2], (IMAGE,), jnp.float32) ** shard_levels(key_of[2], (IMAGE,), ((0, 8),), -0.2, 0.2)), 0.2, 2.0),
        "hadamard_order": jax.random.permutation(key_of[3], SHOT_DEV).astype(jnp.int32),
        "shot_signs": with_ends(jax.random.randint(key_of[4], (SHOT,), 0, 2), jax.random.fold_in(key_of[4], 1), 0, 1).astype(jnp.int32),
    }


def parity(values, bit_count):
    result = jnp.zeros_like(values)
    for shift_by in range(bit_count):
        result = jnp.bitwise_xor(result, jnp.bitwise_and(jnp.right_shift(values, shift_by), 1))
    return result


def reference(shot_green, rec_green, model, hadamard_order, shot_signs):
    columns = jnp.arange(SHOT_DEV, dtype=jnp.int32)
    local_code = (1 - 2 * parity(jnp.bitwise_and(hadamard_order[:, None], columns[None, :]), SHOT_DEV.bit_length() - 1)).astype(jnp.float32)
    block_ids = jnp.arange(N_SHOT, dtype=jnp.int32)
    sylvester = (1 - 2 * parity(jnp.bitwise_and(block_ids[:, None], block_ids[None, :]), N_SHOT.bit_length() - 1)).astype(jnp.float32)
    signs = (1 - 2 * shot_signs).astype(jnp.float32)
    signed_field = (shot_green.astype(jnp.float32) * signs[None, None, :]).reshape(2, IMAGE, N_SHOT, SHOT_DEV)
    coded = jnp.einsum("pxcd,bd->pxcb", signed_field, local_code, precision=lax.Precision.HIGHEST)
    encoded = jnp.einsum("pxcb,ac->pxab", coded, sylvester, precision=lax.Precision.HIGHEST).reshape(2, IMAGE, SHOT)
    scaled = (model[None, :, None] * encoded * (SHOT ** -0.5)).astype(jnp.bfloat16)
    real_part = jnp.dot(rec_green[0], scaled[0], preferred_element_type=jnp.float32) - jnp.dot(rec_green[1], scaled[1], preferred_element_type=jnp.float32)
    imag_part = jnp.dot(rec_green[0], scaled[1], preferred_element_type=jnp.float32) + jnp.dot(rec_green[1], scaled[0], preferred_element_type=jnp.float32)
    return jnp.stack((real_part, imag_part)).astype(jnp.bfloat16)
```

```python
import functools

import jax
import jax.numpy as jnp
from jax import lax
from jax.experimental import pallas as pl
from jax.experimental.pallas import tpu as pltpu
from jax.sharding import PartitionSpec as P

MESH = pl.DeviceIdType.MESH


def parity(values, bit_count):
    shift_by = 1
    while shift_by < bit_count:
        shift_by *= 2
    while shift_by > 1:
        shift_by //= 2
        values = jnp.bitwise_xor(values, jnp.right_shift(values, shift_by))
    return jnp.bitwise_and(values, 1)


def kernel(
    planes,
    chips,
    chunks,
    relayed,
    green_ref,
    rec_hbm,
    model_ref,
    order_ref,
    signs_ref,
    out_ref,
    raw,
    field,
    rec,
    acc,
    code,
    model_col,
    rec_sem,
    raw_send,
    raw_recv,
    field_send,
    field_recv,
):
    blocks = 2 * chips
    img, shot = lax.axis_index("img"), lax.axis_index("shot")
    z, y = img // 2, img % 2
    chip, core = shot // 2, shot % 2
    other_y = 1 - y
    _, _, part_rows, width = field.shape[1:]
    x_local = chunks * part_rows
    has_up, has_down = z < planes - 1, z > 0
    up = (jnp.minimum(z + 1, planes - 1) * 2 + y, shot)
    down = (jnp.maximum(z - 1, 0) * 2 + y, shot)
    across = (z * 2 + other_y, shot)
    sibling = (img, chip * 2 + 1 - core)

    def far(step):
        return (img, lax.rem(chip + step, chips) * 2 + core)

    barrier = pltpu.get_barrier_semaphore()

    def greet(device):
        pl.semaphore_signal(barrier, inc=1, device_id=device, device_id_type=MESH)

    for step in range(1, chips):
        greet(far(step))
    greet(sibling)
    greet(across)
    pl.when(has_up)(lambda: greet(up))
    pl.when(has_down)(lambda: greet(down))

    rec_copy = pltpu.make_async_copy(rec_hbm, rec, rec_sem)
    rec_copy.start()

    signs = (1 - 2 * signs_ref[...]).astype(jnp.float32)
    for j in range(chunks):
        for p in range(2):
            piece = green_ref[p, j * part_rows : (j + 1) * part_rows, :].astype(jnp.float32)
            raw[shot, j, p] = (piece * signs).astype(jnp.bfloat16)

    pl.semaphore_wait(barrier, chips + 1 + has_up.astype(jnp.int32) + has_down.astype(jnp.int32))

    def send_raw(j, step):
        return pltpu.make_async_remote_copy(
            src_ref=raw.at[shot, j],
            dst_ref=raw.at[shot, j],
            send_sem=raw_send.at[0, step, j],
            recv_sem=raw_recv.at[shot, j],
            device_id=sibling if step == 0 else far(step),
            device_id_type=MESH,
        )

    def pass_raw(j, step):
        owner = lax.rem(chip + step, chips) * 2 + core
        return pltpu.make_async_remote_copy(
            src_ref=raw.at[owner, j],
            dst_ref=raw.at[owner, j],
            send_sem=raw_send.at[1, step, j],
            recv_sem=raw_recv.at[owner, j],
            device_id=sibling,
            device_id_type=MESH,
        )

    def got_raw(owner, j):
        pltpu.make_async_remote_copy(
            src_ref=raw.at[owner, j],
            dst_ref=raw.at[owner, j],
            send_sem=raw_send.at[0, 0, j],
            recv_sem=raw_recv.at[owner, j],
            device_id=sibling,
            device_id_type=MESH,
        ).wait_recv()

    for j in range(chunks):
        for step in range(1, chips):
            send_raw(j, step).start()
        send_raw(j, 0).start()

    d_ids = lax.broadcasted_iota(jnp.int32, (width, width), 0)
    bits = parity(jnp.bitwise_and(order_ref[...], d_ids), width.bit_length() - 1)
    code[...] = (1 - 2 * bits).astype(jnp.float32).astype(jnp.bfloat16)
    row_ids = lax.broadcasted_iota(jnp.int32, (x_local, x_local), 0)
    column_ids = lax.broadcasted_iota(jnp.int32, (x_local, x_local), 1)
    model_col[...] = jnp.sum(
        jnp.where(row_ids == column_ids, model_ref[...], 0.0), axis=1, keepdims=True
    )
    acc[...] = jnp.zeros_like(acc)

    def field_copy(way, block, j):
        return pltpu.make_async_remote_copy(
            src_ref=field.at[block, j],
            dst_ref=field.at[block, j],
            send_sem=field_send.at[way, block, j],
            recv_sem=field_recv.at[block, j],
            device_id=(across, up, down)[way],
            device_id_type=MESH,
        )

    def send(way, block, j):
        field_copy(way, block, j).start()

    def got(block, j):
        field_copy(0, block, j).wait_recv()

    def encode(j, carry):
        for step in range(1, chips):
            got_raw(lax.rem(chip + step, chips) * 2 + core, j)
            pass_raw(j, step).start()
        for step in range(chips):
            got_raw(lax.rem(chip + step, chips) * 2 + 1 - core, j)
        encoded = jnp.zeros((2 * part_rows, width), jnp.float32)
        for c in range(blocks):
            coded = jnp.dot(
                raw[c, j].reshape(2 * part_rows, width),
                code[...],
                preferred_element_type=jnp.float32,
            )
            flip = parity(jnp.bitwise_and(shot, c), blocks.bit_length() - 1)
            encoded += (1 - 2 * flip).astype(jnp.float32) * coded
        rows = pl.multiple_of(j * part_rows, 16)
        model = model_col[pl.ds(rows, part_rows), :]
        for p in range(2):
            scaled = model * encoded[p * part_rows : (p + 1) * part_rows] * (blocks * width) ** (-0.5)
            field[img, j, p] = scaled.astype(jnp.bfloat16)
        send(0, img, j)
        pl.when(has_up)(lambda: send(1, img, j))
        pl.when(has_down)(lambda: send(2, img, j))

        @pl.when(j >= chunks - relayed)
        def _():
            block, k = z * 2 + other_y, j - (chunks - relayed)
            got(block, k)
            pl.when(has_up)(lambda: send(1, block, k))
            pl.when(has_down)(lambda: send(2, block, k))

        return carry

    lax.fori_loop(0, chunks, encode, 0)
    rec_copy.wait()

    def multiply(plane):
        columns = pl.ds(pl.multiple_of(plane * (2 * x_local), 128), 2 * x_local)
        parts = [
            field[pl.ds(plane * 2, 2), :, p].reshape(2 * x_local, width) for p in range(2)
        ]

        def product(q, p):
            return jnp.dot(rec[q, :, columns], parts[p], preferred_element_type=jnp.float32)

        acc[0] += product(0, 0) - product(1, 1)
        acc[1] += product(0, 1) + product(1, 0)

    def at_distance(s, carry):
        ways = ((z - s, z - s >= 0, has_up, 1), (z + s, z + s < planes, has_down, 2))

        def arrive(j, inner):
            for plane, there, onward, way in ways:

                @pl.when(there)
                def _():
                    block = plane * 2 + y
                    got(block, j)
                    pl.when(onward)(lambda: send(way, block, j))
                    pl.when(j >= relayed)(lambda: send(0, block, j))

                @pl.when(there & (j >= chunks - relayed))
                def _():
                    block, k = plane * 2 + other_y, j - (chunks - relayed)
                    got(block, k)
                    pl.when(onward)(lambda: send(way, block, k))

            return inner

        lax.fori_loop(0, chunks, arrive, 0)

        def nearer(which, inner):
            plane = z + (2 * which - 1) * (s - 1)

            @pl.when((plane >= 0) & (plane < planes) & ((s > 1) | (which == 0)))
            def _():
                def wait(j, nothing):
                    got(plane * 2 + other_y, j)
                    return nothing

                lax.fori_loop(relayed, chunks, wait, 0)
                multiply(plane)

            return inner

        lax.fori_loop(0, 2, nearer, 0)
        return carry

    lax.fori_loop(1, planes + 1, at_distance, 0)
    out_ref[...] = acc[...].astype(out_ref.dtype)

    def left_raw(j, carry):
        for step in range(chips):
            send_raw(j, step).wait_send()
        for step in range(1, chips):
            pass_raw(j, step).wait_send()
        return carry

    lax.fori_loop(0, chunks, left_raw, 0)

    def left_field(plane, carry):
        from_below, from_above = plane <= z, plane >= z

        def chunk(j, inner):
            near, opposite = plane * 2 + y, plane * 2 + other_y
            pl.when((j >= relayed) | (plane == z))(lambda: field_copy(0, near, j).wait_send())
            pl.when(from_below & has_up)(lambda: field_copy(1, near, j).wait_send())
            pl.when(from_above & has_down)(lambda: field_copy(2, near, j).wait_send())
            pl.when((j < relayed) & from_below & has_up)(
                lambda: field_copy(1, opposite, j).wait_send()
            )
            pl.when((j < relayed) & from_above & has_down)(
                lambda: field_copy(2, opposite, j).wait_send()
            )
            return inner

        lax.fori_loop(0, chunks, chunk, 0)
        return carry

    lax.fori_loop(0, planes, left_field, 0)


def on_device(shot_green, rec_green, model, hadamard_order, shot_signs):
    _, x_local, width = shot_green.shape
    planes = lax.axis_size("img") // 2
    chips = lax.axis_size("shot") // 2
    chunks = max(n for n in range(1, 9) if x_local % (16 * n) == 0)
    relayed = 1 if chunks > 2 else 0
    part_rows = x_local // chunks
    in_vmem = pl.BlockSpec(memory_space=pltpu.VMEM)
    return pl.pallas_call(
        functools.partial(kernel, planes, chips, chunks, relayed),
        out_shape=jax.ShapeDtypeStruct((2, x_local, width), jnp.bfloat16),
        in_specs=[in_vmem, pl.BlockSpec(memory_space=pl.ANY), in_vmem, in_vmem, in_vmem],
        out_specs=in_vmem,
        scratch_shapes=[
            pltpu.VMEM((2 * chips, chunks, 2, part_rows, width), jnp.bfloat16),
            pltpu.VMEM((2 * planes, chunks, 2, part_rows, width), jnp.bfloat16),
            pltpu.VMEM(rec_green.shape, jnp.bfloat16),
            pltpu.VMEM((2, x_local, width), jnp.float32),
            pltpu.VMEM((width, width), jnp.bfloat16),
            pltpu.VMEM((x_local, 1), jnp.float32),
            pltpu.SemaphoreType.DMA,
            pltpu.SemaphoreType.DMA((2, chips, chunks)),
            pltpu.SemaphoreType.DMA((2 * chips, chunks)),
            pltpu.SemaphoreType.DMA((3, 2 * planes, chunks)),
            pltpu.SemaphoreType.DMA((2 * planes, chunks)),
        ],
        compiler_params=pltpu.CompilerParams(
            collective_id=0, has_side_effects=True, vmem_limit_bytes=48 * 2**20
        ),
        cost_estimate=pl.CostEstimate(
            flops=8 * x_local * rec_green.shape[2] * width,
            bytes_accessed=rec_green.size * 2,
            transcendentals=0,
        ),
    )(
        shot_green,
        rec_green,
        model.reshape(1, x_local),
        hadamard_order.reshape(1, width),
        shot_signs.reshape(1, width),
    )


def solution(mesh):
    placed = (P(None, "img", "shot"), P(None, "img", None), P("img"), P(), P("shot"))
    return jax.shard_map(
        on_device, mesh=mesh, in_specs=placed, out_specs=P(None, "img", "shot"), check_vma=False
    )
```

```python
import functools

import jax
import jax.numpy as jnp
from jax import lax
from jax.experimental import pallas as pl
from jax.experimental.pallas import tpu as pltpu
from jax.sharding import PartitionSpec as P

MESH = pl.DeviceIdType.MESH


def parity(values, bit_count):
    shift_by = 1
    while shift_by < bit_count:
        shift_by *= 2
    while shift_by > 1:
        shift_by //= 2
        values = jnp.bitwise_xor(values, jnp.right_shift(values, shift_by))
    return jnp.bitwise_and(values, 1)


def kernel(
    planes,
    chips,
    chunks,
    relayed,
    green_hbm,
    rec_hbm,
    model_hbm,
    order_hbm,
    signs_hbm,
    out_ref,
    green_ref,
    model_ref,
    order_ref,
    signs_ref,
    raw,
    field,
    rec,
    acc,
    code,
    model_col,
    load_sem,
    raw_send,
    raw_recv,
    field_send,
    field_recv,
):
    blocks = 2 * chips
    img, shot = lax.axis_index("img"), lax.axis_index("shot")
    z, y = img // 2, img % 2
    chip, core = shot // 2, shot % 2
    other_y = 1 - y
    _, _, part_rows, width = field.shape[1:]
    x_local = chunks * part_rows
    has_up, has_down = z < planes - 1, z > 0
    up = (jnp.minimum(z + 1, planes - 1) * 2 + y, shot)
    down = (jnp.maximum(z - 1, 0) * 2 + y, shot)
    across = (z * 2 + other_y, shot)
    sibling = (img, chip * 2 + 1 - core)

    def far(step):
        return (img, lax.rem(chip + step, chips) * 2 + core)

    loads = [
        pltpu.make_async_copy(source, target, load_sem.at[n])
        for n, (source, target) in enumerate(
            (
                (signs_hbm, signs_ref),
                (green_hbm, green_ref),
                (order_hbm, order_ref),
                (model_hbm, model_ref),
                (rec_hbm, rec),
            )
        )
    ]

    barrier = pltpu.get_barrier_semaphore()

    def greet(device):
        pl.semaphore_signal(barrier, inc=1, device_id=device, device_id_type=MESH)

    for step in range(1, chips):
        greet(far(step))
    greet(sibling)
    greet(across)
    pl.when(has_up)(lambda: greet(up))
    pl.when(has_down)(lambda: greet(down))

    for load in loads:
        load.start()
    for load in loads[:2]:
        load.wait()

    signs = (1 - 2 * signs_ref[...]).astype(jnp.float32)
    for j in range(chunks):
        for p in range(2):
            piece = green_ref[p, j * part_rows : (j + 1) * part_rows, :].astype(jnp.float32)
            raw[shot, j, p] = (piece * signs).astype(jnp.bfloat16)

    pl.semaphore_wait(barrier, chips + 1 + has_up.astype(jnp.int32) + has_down.astype(jnp.int32))

    def send_raw(j, step):
        return pltpu.make_async_remote_copy(
            src_ref=raw.at[shot, j],
            dst_ref=raw.at[shot, j],
            send_sem=raw_send.at[0, step],
            recv_sem=raw_recv.at[shot, j],
            device_id=sibling if step == 0 else far(step),
            device_id_type=MESH,
        )

    def pass_raw(j, step):
        owner = lax.rem(chip + step, chips) * 2 + core
        return pltpu.make_async_remote_copy(
            src_ref=raw.at[owner, j],
            dst_ref=raw.at[owner, j],
            send_sem=raw_send.at[1, step],
            recv_sem=raw_recv.at[owner, j],
            device_id=sibling,
            device_id_type=MESH,
        )

    def got_raw(owner, j):
        pltpu.make_async_remote_copy(
            src_ref=raw.at[owner, j],
            dst_ref=raw.at[owner, j],
            send_sem=raw_send.at[0, 0],
            recv_sem=raw_recv.at[owner, j],
            device_id=sibling,
            device_id_type=MESH,
        ).wait_recv()

    for j in range(chunks):
        for step in range(1, chips):
            send_raw(j, step).start()
        send_raw(j, 0).start()

    for load in loads[2:4]:
        load.wait()

    d_ids = lax.broadcasted_iota(jnp.int32, (width, width), 0)
    bits = parity(jnp.bitwise_and(order_ref[...], d_ids), width.bit_length() - 1)
    code[...] = (1 - 2 * bits).astype(jnp.float32).astype(jnp.bfloat16)
    row_ids = lax.broadcasted_iota(jnp.int32, (x_local, x_local), 0)
    column_ids = lax.broadcasted_iota(jnp.int32, (x_local, x_local), 1)
    model_col[...] = jnp.sum(
        jnp.where(row_ids == column_ids, model_ref[...], 0.0), axis=1, keepdims=True
    )
    acc[...] = jnp.zeros_like(acc)

    def field_copy(way, block, j):
        return pltpu.make_async_remote_copy(
            src_ref=field.at[block, j],
            dst_ref=field.at[block, j],
            send_sem=field_send.at[way, block],
            recv_sem=field_recv.at[block, j],
            device_id=(across, up, down)[way],
            device_id_type=MESH,
        )

    def send(way, block, j):
        field_copy(way, block, j).start()

    def got(block, j):
        field_copy(0, block, j).wait_recv()

    def relay_raw(j):
        for step in range(1, chips):
            got_raw(lax.rem(chip + step, chips) * 2 + core, j)
            pass_raw(j, step).start()

    relay_raw(0)

    def encode(j, carry):
        pl.when(j + 1 < chunks)(lambda: relay_raw(j + 1))
        for step in range(chips):
            got_raw(lax.rem(chip + step, chips) * 2 + 1 - core, j)
        all_coded = jnp.dot(
            raw[:, j].reshape(blocks * 2 * part_rows, width),
            code[...],
            preferred_element_type=jnp.float32,
        )
        encoded = jnp.zeros((2 * part_rows, width), jnp.float32)
        for c in range(blocks):
            coded = all_coded[c * 2 * part_rows : (c + 1) * 2 * part_rows]
            flip = parity(jnp.bitwise_and(shot, c), blocks.bit_length() - 1)
            encoded += (1 - 2 * flip).astype(jnp.float32) * coded
        rows = pl.multiple_of(j * part_rows, 16)
        model = model_col[pl.ds(rows, part_rows), :]
        for p in range(2):
            scaled = model * encoded[p * part_rows : (p + 1) * part_rows] * (blocks * width) ** (-0.5)
            field[img, j, p] = scaled.astype(jnp.bfloat16)
        send(0, img, j)
        pl.when(has_up)(lambda: send(1, img, j))
        pl.when(has_down)(lambda: send(2, img, j))

        @pl.when(j >= chunks - relayed)
        def _():
            block, k = z * 2 + other_y, j - (chunks - relayed)
            got(block, k)
            pl.when(has_up)(lambda: send(1, block, k))
            pl.when(has_down)(lambda: send(2, block, k))

        return carry

    lax.fori_loop(0, chunks, encode, 0)
    loads[4].wait()

    def multiply(plane):
        columns = pl.ds(pl.multiple_of(plane * (2 * x_local), 128), 2 * x_local)
        parts = [
            field[pl.ds(plane * 2, 2), :, p].reshape(2 * x_local, width) for p in range(2)
        ]

        def product(q, p):
            return jnp.dot(rec[q, :, columns], parts[p], preferred_element_type=jnp.float32)

        acc[0] += product(0, 0) - product(1, 1)
        acc[1] += product(0, 1) + product(1, 0)

    def left(buffer, semaphore):
        pltpu.make_async_remote_copy(
            src_ref=buffer,
            dst_ref=buffer,
            send_sem=semaphore,
            recv_sem=field_recv.at[0, 0],
            device_id=sibling,
            device_id_type=MESH,
        ).wait_send()

    def left_raw():
        for step in range(chips):
            left(raw.at[shot], raw_send.at[0, step])
        for step in range(1, chips):
            left(raw.at[lax.rem(chip + step, chips) * 2 + core], raw_send.at[1, step])

    def left_field(plane, carry):
        from_below, from_above = plane <= z, plane >= z
        near, opposite = plane * 2 + y, plane * 2 + other_y
        if relayed:
            pl.when(plane == z)(lambda: left(field.at[near], field_send.at[0, near]))
            pl.when(plane != z)(
                lambda: left(field.at[near, pl.ds(relayed, chunks - relayed)], field_send.at[0, near])
            )
        else:
            left(field.at[near], field_send.at[0, near])
        for goes, way in ((from_below & has_up, 1), (from_above & has_down, 2)):

            @pl.when(goes)
            def _():
                left(field.at[near], field_send.at[way, near])
                if relayed:
                    left(field.at[opposite, pl.ds(0, relayed)], field_send.at[way, opposite])

        return carry

    def at_distance(s, carry):
        ways = ((z - s, z - s >= 0, has_up, 1), (z + s, z + s < planes, has_down, 2))

        def arrive(j, inner):
            for plane, there, onward, way in ways:

                @pl.when(there)
                def _():
                    block = plane * 2 + y
                    got(block, j)
                    pl.when(onward)(lambda: send(way, block, j))
                    pl.when(j >= relayed)(lambda: send(0, block, j))

                @pl.when(there & (j >= chunks - relayed))
                def _():
                    block, k = plane * 2 + other_y, j - (chunks - relayed)
                    got(block, k)
                    pl.when(onward)(lambda: send(way, block, k))

            return inner

        lax.fori_loop(0, chunks, arrive, 0)

        @pl.when(s == planes)
        def _():
            left_raw()
            lax.fori_loop(0, planes, left_field, 0)

        def nearer(which, inner):
            plane = z + (2 * which - 1) * (s - 1)

            @pl.when((plane >= 0) & (plane < planes) & ((s > 1) | (which == 0)))
            def _():
                def wait(j, nothing):
                    got(plane * 2 + other_y, j)
                    return nothing

                lax.fori_loop(relayed, chunks, wait, 0)
                multiply(plane)

            return inner

        lax.fori_loop(0, 2, nearer, 0)
        return carry

    lax.fori_loop(1, planes + 1, at_distance, 0)
    out_ref[...] = acc[...].astype(out_ref.dtype)


def on_device(shot_green, rec_green, model, hadamard_order, shot_signs):
    _, x_local, width = shot_green.shape
    planes = lax.axis_size("img") // 2
    chips = lax.axis_size("shot") // 2
    chunks = max(n for n in range(1, 9) if x_local % (16 * n) == 0)
    relayed = 1 if chunks > 2 else 0
    part_rows = x_local // chunks
    in_hbm = pl.BlockSpec(memory_space=pltpu.HBM)
    return pl.pallas_call(
        functools.partial(kernel, planes, chips, chunks, relayed),
        out_shape=jax.ShapeDtypeStruct((2, x_local, width), jnp.bfloat16),
        in_specs=[in_hbm] * 5,
        out_specs=pl.BlockSpec(memory_space=pltpu.VMEM),
        scratch_shapes=[
            pltpu.VMEM(shot_green.shape, jnp.bfloat16),
            pltpu.VMEM((1, x_local), jnp.float32),
            pltpu.VMEM((1, width), jnp.int32),
            pltpu.VMEM((1, width), jnp.int32),
            pltpu.VMEM((2 * chips, chunks, 2, part_rows, width), jnp.bfloat16),
            pltpu.VMEM((2 * planes, chunks, 2, part_rows, width), jnp.bfloat16),
            pltpu.VMEM(rec_green.shape, jnp.bfloat16),
            pltpu.VMEM((2, x_local, width), jnp.float32),
            pltpu.VMEM((width, width), jnp.bfloat16),
            pltpu.VMEM((x_local, 1), jnp.float32),
            pltpu.SemaphoreType.DMA((5,)),
            pltpu.SemaphoreType.DMA((2, chips)),
            pltpu.SemaphoreType.DMA((2 * chips, chunks)),
            pltpu.SemaphoreType.DMA((3, 2 * planes)),
            pltpu.SemaphoreType.DMA((2 * planes, chunks)),
        ],
        compiler_params=pltpu.CompilerParams(
            collective_id=0, has_side_effects=True, vmem_limit_bytes=48 * 2**20
        ),
        cost_estimate=pl.CostEstimate(
            flops=8 * x_local * rec_green.shape[2] * width,
            bytes_accessed=rec_green.size * 2,
            transcendentals=0,
        ),
    )(
        shot_green,
        rec_green,
        model.reshape(1, x_local),
        hadamard_order.reshape(1, width),
        shot_signs.reshape(1, width),
    )


def solution(mesh):
    placed = (P(None, "img", "shot"), P(None, "img", None), P("img"), P(), P("shot"))
    return jax.shard_map(
        on_device, mesh=mesh, in_specs=placed, out_specs=P(None, "img", "shot"), check_vma=False
    )
```

```python
import functools

import jax
import jax.numpy as jnp
from jax import lax
from jax.experimental import pallas as pl
from jax.experimental.pallas import tpu as pltpu
from jax.sharding import PartitionSpec as P

MESH = pl.DeviceIdType.MESH


def parity(values, bit_count):
    shift_by = 1
    while shift_by < bit_count:
        shift_by *= 2
    while shift_by > 1:
        shift_by //= 2
        values = jnp.bitwise_xor(values, jnp.right_shift(values, shift_by))
    return jnp.bitwise_and(values, 1)


def kernel(
    planes,
    chips,
    chunks,
    relayed,
    green_hbm,
    rec_hbm,
    model_hbm,
    order_hbm,
    signs_hbm,
    out_ref,
    green_ref,
    model_ref,
    order_ref,
    signs_ref,
    raw,
    field,
    rec,
    acc,
    code,
    model_col,
    load_sem,
    raw_send,
    raw_recv,
    field_send,
    field_recv,
    across_recv,
):
    blocks = 2 * chips
    img, shot = lax.axis_index("img"), lax.axis_index("shot")
    z, y = img // 2, img % 2
    chip, core = shot // 2, shot % 2
    other_y = 1 - y
    _, _, part_rows, width = field.shape[1:]
    x_local = chunks * part_rows
    has_up, has_down = z < planes - 1, z > 0
    up = (jnp.minimum(z + 1, planes - 1) * 2 + y, shot)
    down = (jnp.maximum(z - 1, 0) * 2 + y, shot)
    across = (z * 2 + other_y, shot)
    sibling = (img, chip * 2 + 1 - core)

    def far(step):
        return (img, lax.rem(chip + step, chips) * 2 + core)

    loads = [
        pltpu.make_async_copy(source, target, load_sem.at[n])
        for n, (source, target) in enumerate(
            (
                (signs_hbm, signs_ref),
                (green_hbm, green_ref),
                (order_hbm, order_ref),
                (model_hbm, model_ref),
                (rec_hbm, rec),
            )
        )
    ]

    barrier = pltpu.get_barrier_semaphore()

    def greet(device):
        pl.semaphore_signal(barrier, inc=1, device_id=device, device_id_type=MESH)

    for step in range(1, chips):
        greet(far(step))
    greet(sibling)
    greet(across)
    pl.when(has_up)(lambda: greet(up))
    pl.when(has_down)(lambda: greet(down))

    for load in loads:
        load.start()
    for load in loads[:2]:
        load.wait()

    signs = (1 - 2 * signs_ref[...]).astype(jnp.float32)
    for j in range(chunks):
        for p in range(2):
            piece = green_ref[p, j * part_rows : (j + 1) * part_rows, :].astype(jnp.float32)
            raw[shot, j, p] = (piece * signs).astype(jnp.bfloat16)

    pl.semaphore_wait(barrier, chips + 1 + has_up.astype(jnp.int32) + has_down.astype(jnp.int32))

    def send_raw(j, step):
        return pltpu.make_async_remote_copy(
            src_ref=raw.at[shot, j],
            dst_ref=raw.at[shot, j],
            send_sem=raw_send.at[0, step],
            recv_sem=raw_recv.at[shot, j],
            device_id=sibling if step == 0 else far(step),
            device_id_type=MESH,
        )

    def pass_raw(j, step):
        owner = lax.rem(chip + step, chips) * 2 + core
        return pltpu.make_async_remote_copy(
            src_ref=raw.at[owner, j],
            dst_ref=raw.at[owner, j],
            send_sem=raw_send.at[1, step],
            recv_sem=raw_recv.at[owner, j],
            device_id=sibling,
            device_id_type=MESH,
        )

    def got_raw(owner, j):
        pltpu.make_async_remote_copy(
            src_ref=raw.at[owner, j],
            dst_ref=raw.at[owner, j],
            send_sem=raw_send.at[0, 0],
            recv_sem=raw_recv.at[owner, j],
            device_id=sibling,
            device_id_type=MESH,
        ).wait_recv()

    for j in range(chunks):
        for step in range(1, chips):
            send_raw(j, step).start()
        send_raw(j, 0).start()

    for load in loads[2:4]:
        load.wait()

    d_ids = lax.broadcasted_iota(jnp.int32, (width, width), 0)
    bits = parity(jnp.bitwise_and(order_ref[...], d_ids), width.bit_length() - 1)
    code[...] = (1 - 2 * bits).astype(jnp.float32).astype(jnp.bfloat16)
    row_ids = lax.broadcasted_iota(jnp.int32, (x_local, x_local), 0)
    column_ids = lax.broadcasted_iota(jnp.int32, (x_local, x_local), 1)
    model_col[...] = jnp.sum(
        jnp.where(row_ids == column_ids, model_ref[...], 0.0), axis=1, keepdims=True
    )
    acc[...] = jnp.zeros_like(acc)

    def field_copy(way, block, j):
        return pltpu.make_async_remote_copy(
            src_ref=field.at[block, j],
            dst_ref=field.at[block, j],
            send_sem=field_send.at[way, block],
            recv_sem=field_recv.at[block, j],
            device_id=(across, up, down)[way],
            device_id_type=MESH,
        )

    def send_across(block, j):
        pltpu.make_async_remote_copy(
            src_ref=field.at[block, j],
            dst_ref=field.at[block, j],
            send_sem=field_send.at[0, block],
            recv_sem=across_recv.at[block],
            device_id=across,
            device_id_type=MESH,
        ).start()

    def send(way, block, j):
        field_copy(way, block, j).start()

    def got(block, j):
        field_copy(0, block, j).wait_recv()

    def relay_raw(j):
        for step in range(1, chips):
            got_raw(lax.rem(chip + step, chips) * 2 + core, j)
            pass_raw(j, step).start()

    relay_raw(0)

    def encode(j, carry):
        pl.when(j + 1 < chunks)(lambda: relay_raw(j + 1))
        for step in range(chips):
            got_raw(lax.rem(chip + step, chips) * 2 + 1 - core, j)
        all_coded = jnp.dot(
            raw[:, j].reshape(blocks * 2 * part_rows, width),
            code[...],
            preferred_element_type=jnp.float32,
        )
        encoded = jnp.zeros((2 * part_rows, width), jnp.float32)
        for c in range(blocks):
            coded = all_coded[c * 2 * part_rows : (c + 1) * 2 * part_rows]
            flip = parity(jnp.bitwise_and(shot, c), blocks.bit_length() - 1)
            encoded += (1 - 2 * flip).astype(jnp.float32) * coded
        rows = pl.multiple_of(j * part_rows, 16)
        model = model_col[pl.ds(rows, part_rows), :]
        for p in range(2):
            scaled = model * encoded[p * part_rows : (p + 1) * part_rows] * (blocks * width) ** (-0.5)
            field[img, j, p] = scaled.astype(jnp.bfloat16)
        pl.when(j < relayed)(lambda: send(0, img, j))
        pl.when(j >= relayed)(lambda: send_across(img, j))
        pl.when(has_up)(lambda: send(1, img, j))
        pl.when(has_down)(lambda: send(2, img, j))

        @pl.when(j >= chunks - relayed)
        def _():
            block, k = z * 2 + other_y, j - (chunks - relayed)
            got(block, k)
            pl.when(has_up)(lambda: send(1, block, k))
            pl.when(has_down)(lambda: send(2, block, k))

        return carry

    lax.fori_loop(0, chunks, encode, 0)
    loads[4].wait()

    def multiply(plane):
        columns = pl.ds(pl.multiple_of(plane * (2 * x_local), 128), 2 * x_local)
        parts = [
            field[pl.ds(plane * 2, 2), :, p].reshape(2 * x_local, width) for p in range(2)
        ]

        def product(q, p):
            return jnp.dot(rec[q, :, columns], parts[p], preferred_element_type=jnp.float32)

        acc[0] += product(0, 0) - product(1, 1)
        acc[1] += product(0, 1) + product(1, 0)

    def left(buffer, semaphore):
        pltpu.make_async_remote_copy(
            src_ref=buffer,
            dst_ref=buffer,
            send_sem=semaphore,
            recv_sem=field_recv.at[0, 0],
            device_id=sibling,
            device_id_type=MESH,
        ).wait_send()

    def left_raw():
        for step in range(chips):
            left(raw.at[shot], raw_send.at[0, step])
        for step in range(1, chips):
            left(raw.at[lax.rem(chip + step, chips) * 2 + core], raw_send.at[1, step])

    def left_field(plane, carry):
        from_below, from_above = plane <= z, plane >= z
        near, opposite = plane * 2 + y, plane * 2 + other_y
        if relayed:
            pl.when(plane == z)(lambda: left(field.at[near], field_send.at[0, near]))
            pl.when(plane != z)(
                lambda: left(field.at[near, pl.ds(relayed, chunks - relayed)], field_send.at[0, near])
            )
        else:
            left(field.at[near], field_send.at[0, near])
        for goes, way in ((from_below & has_up, 1), (from_above & has_down, 2)):

            @pl.when(goes)
            def _():
                left(field.at[near], field_send.at[way, near])
                if relayed:
                    left(field.at[opposite, pl.ds(0, relayed)], field_send.at[way, opposite])

        return carry

    def at_distance(s, carry):
        ways = ((z - s, z - s >= 0, has_up, 1), (z + s, z + s < planes, has_down, 2))

        def arrive(j, inner):
            for plane, there, onward, way in ways:

                @pl.when(there)
                def _():
                    block = plane * 2 + y
                    got(block, j)
                    pl.when(onward)(lambda: send(way, block, j))
                    pl.when(j >= relayed)(lambda: send_across(block, j))

                @pl.when(there & (j >= chunks - relayed))
                def _():
                    block, k = plane * 2 + other_y, j - (chunks - relayed)
                    got(block, k)
                    pl.when(onward)(lambda: send(way, block, k))

            return inner

        lax.fori_loop(0, chunks, arrive, 0)

        @pl.when(s == planes)
        def _():
            left_raw()
            lax.fori_loop(0, planes, left_field, 0)

        def nearer(which, inner):
            plane = z + (2 * which - 1) * (s - 1)

            @pl.when((plane >= 0) & (plane < planes) & ((s > 1) | (which == 0)))
            def _():
                block = plane * 2 + other_y
                rest = field.at[block, pl.ds(relayed, chunks - relayed)]
                pltpu.make_async_remote_copy(
                    src_ref=rest,
                    dst_ref=rest,
                    send_sem=field_send.at[0, block],
                    recv_sem=across_recv.at[block],
                    device_id=across,
                    device_id_type=MESH,
                ).wait_recv()
                multiply(plane)

            return inner

        lax.fori_loop(0, 2, nearer, 0)
        return carry

    lax.fori_loop(1, planes + 1, at_distance, 0)
    out_ref[...] = acc[...].astype(out_ref.dtype)


def on_device(shot_green, rec_green, model, hadamard_order, shot_signs):
    _, x_local, width = shot_green.shape
    planes = lax.axis_size("img") // 2
    chips = lax.axis_size("shot") // 2
    chunks = max(n for n in range(1, 9) if x_local % (16 * n) == 0)
    relayed = 1 if chunks > 2 else 0
    part_rows = x_local // chunks
    in_hbm = pl.BlockSpec(memory_space=pltpu.HBM)
    return pl.pallas_call(
        functools.partial(kernel, planes, chips, chunks, relayed),
        out_shape=jax.ShapeDtypeStruct((2, x_local, width), jnp.bfloat16),
        in_specs=[in_hbm] * 5,
        out_specs=pl.BlockSpec(memory_space=pltpu.VMEM),
        scratch_shapes=[
            pltpu.VMEM(shot_green.shape, jnp.bfloat16),
            pltpu.VMEM((1, x_local), jnp.float32),
            pltpu.VMEM((1, width), jnp.int32),
            pltpu.VMEM((1, width), jnp.int32),
            pltpu.VMEM((2 * chips, chunks, 2, part_rows, width), jnp.bfloat16),
            pltpu.VMEM((2 * planes, chunks, 2, part_rows, width), jnp.bfloat16),
            pltpu.VMEM(rec_green.shape, jnp.bfloat16),
            pltpu.VMEM((2, x_local, width), jnp.float32),
            pltpu.VMEM((width, width), jnp.bfloat16),
            pltpu.VMEM((x_local, 1), jnp.float32),
            pltpu.SemaphoreType.DMA((5,)),
            pltpu.SemaphoreType.DMA((2, chips)),
            pltpu.SemaphoreType.DMA((2 * chips, chunks)),
            pltpu.SemaphoreType.DMA((3, 2 * planes)),
            pltpu.SemaphoreType.DMA((2 * planes, chunks)),
            pltpu.SemaphoreType.DMA((2 * planes,)),
        ],
        compiler_params=pltpu.CompilerParams(
            collective_id=0, has_side_effects=True, vmem_limit_bytes=48 * 2**20
        ),
        cost_estimate=pl.CostEstimate(
            flops=8 * x_local * rec_green.shape[2] * width,
            bytes_accessed=rec_green.size * 2,
            transcendentals=0,
        ),
    )(
        shot_green,
        rec_green,
        model.reshape(1, x_local),
        hadamard_order.reshape(1, width),
        shot_signs.reshape(1, width),
    )


def solution(mesh):
    placed = (P(None, "img", "shot"), P(None, "img", None), P("img"), P(), P("shot"))
    return jax.shard_map(
        on_device, mesh=mesh, in_specs=placed, out_specs=P(None, "img", "shot"), check_vma=False
    )
```
